32 devices in a mesh: shard: 2 (over core), replica: 16 (over z, y, x).
Axes of the slice: x: 2, y: 2, z: 4, core: 2. Of those that a mesh axis runs over, the one named last changes fastest.
Arguments:
- tokens: bfloat16 [16, 1024, 1088], P('replica', 'shard'), may hold values from -6 to 6
- documents: int32 [16, 1024], P('replica', 'shard'), may hold values from 0 to 2, as said below
- cotangent: bfloat16 [16, 1024, 1088], P('replica', 'shard'), may hold values from -6 to 6
- w_qkv: bfloat16 [1088, 3264], P('shard'), may hold values from -0.1875 to 0.1875
- w_out: bfloat16 [1088, 1088], P('shard'), may hold values from -1.5 to 1.5
- w_up: bfloat16 [1088, 4352], P('shard'), may hold values from -0.1875 to 0.1875
- w_down: bfloat16 [4352, 1088], P('shard'), may hold values from -0.09375 to 0.09375
- gain_one: bfloat16 [1088], P('shard'), may hold values from 0.25 to 1.75
- shift_one: bfloat16 [1088], P('shard'), may hold values from -4 to 4
- bias_query: bfloat16 [1088], P('shard'), may hold values from -4 to 4
- bias_value: bfloat16 [1088], P('shard'), may hold values from -4 to 4
- bias_out: bfloat16 [1088], P('shard'), may hold values from -4 to 4
- gain_two: bfloat16 [1088], P('shard'), may hold values from 0.25 to 1.75
- shift_two: bfloat16 [1088], P('shard'), may hold values from -4 to 4
- bias_up: bfloat16 [4352], P('shard'), may hold values from -4 to 4
- bias_down: bfloat16 [1088], P('shard'), may hold values from -4 to 4
Outputs:
- output: bfloat16 [16, 1024, 1088], P('replica', 'shard')
- input_grad: bfloat16 [16, 1024, 1088], P('replica', 'shard')
- grad_w_qkv: float32 [1088, 3264], P('shard')
- grad_w_out: float32 [1088, 1088], P('shard')
- grad_w_up: float32 [1088, 4352], P('shard')
- grad_w_down: float32 [4352, 1088], P('shard')
- grad_gain_one: float32 [1088], P('shard')
- grad_shift_one: float32 [1088], P('shard')
- grad_bias_query: float32 [1088], P('shard')
- grad_bias_value: float32 [1088], P('shard')
- grad_bias_out: float32 [1088], P('shard')
- grad_gain_two: float32 [1088], P('shard')
- grad_shift_two: float32 [1088], P('shard')
- grad_bias_up: float32 [4352], P('shard')
- grad_bias_down: float32 [1088], P('shard')
The draws below stay inside these ranges and needn't reach their ends.
Inputs may be any that keep to these rules, and one draw needn't show every extreme that they name: Each sequence holds three documents whose numbers never fall; each has 128 tokens or more, and document 1 covers positions 511 and 512.
All inputs are finite; a program needn't handle non-finite values.
Results may differ from the reference program's by a relative error of at most 0.012.
Values may be sent and summed in bfloat16 or wider, within the bound.
No kernel may reach another device: no remote copies, remote signals or barrier semaphores. Data moves between devices by JAX's collectives and lax.ppermute only.
A program may use at most 320 MiB of HBM per device.

```python
import jax
import jax.numpy as jnp
from jax import lax

D = 1088
HEADS = 17
HDIM = 64
FF = 4352
LENGTH = 1024
SEQS = 16


def draw_documents(key, part):
    key = jax.random.fold_in(key, 7)
    early_key, later_key = jax.random.split(key)
    early_cut = jax.random.randint(early_key, (SEQS, 1), LENGTH // 8, 3 * LENGTH // 8)
    later_cut = jax.random.randint(later_key, (SEQS, 1), 5 * LENGTH // 8, 7 * LENGTH // 8)
    places = jnp.arange(LENGTH, dtype=jnp.int32)[None, :]
    return (places >= early_cut).astype(jnp.int32) + (places >= later_cut).astype(jnp.int32)


def shard_levels(own_key, dims, shards, least, largest):
    gain, own = 1.0, jax.random.fold_in(own_key, 6)
    for axis_at, blocks in shards:
        steps = jnp.exp(jax.random.uniform(jax.random.fold_in(own, axis_at), (blocks,), jnp.float32, least / len(shards), largest / len(shards)))
        gain = gain * jnp.repeat(steps, dims[axis_at] // blocks).reshape([-1 if axis == axis_at else 1 for axis in range(len(dims))])
    return gain


def noise(stream_key, shape, deviation, bound, shards=(), kind=jnp.bfloat16):
    level = shard_levels(stream_key, shape, shards, -0.22, 0.18) if shards else 1.0
    values = jax.random.normal(stream_key, shape, jnp.float32) * deviation * level
    return jnp.minimum(jnp.maximum(values, -bound), bound).astype(kind)


def setup_inputs(seed: int = 0) -> dict:
    key_list = jax.random.split(jax.random.key(seed), 17)
    tokens = noise(key_list[0], (SEQS, LENGTH, D), 1.0, 6.0, ((0, 16), (1, 2)))
    documents = draw_documents(jax.random.fold_in(key_list[16], 71), 0)
    cotangent = noise(key_list[2], (SEQS, LENGTH, D), 1.0, 6.0, ((0, 16), (1, 2)))
    w_qkv = noise(key_list[3], (D, 3 * D), D ** -0.5, 0.1875, ((0, 2),))
    w_out = noise(key_list[4], (D, D), (D // 64) ** -0.5, 1.5, ((0, 2),))
    w_up = noise(key_list[5], (D, FF), D ** -0.5, 0.1875, ((0, 2),))
    w_down = noise(key_list[6], (FF, D), FF ** -0.5, 0.09375, ((0, 2),))
    gain_one = jnp.clip(1.0 + 0.15 * jax.random.normal(key_list[7], (D,), jnp.float32), 0.25, 1.75).astype(jnp.bfloat16)
    shift_one = noise(key_list[8], (D,), 0.3, 4.0, ((0, 2),))
    bias_query = noise(key_list[9], (D,), 0.5, 4.0, ((0, 2),))
    bias_value = noise(key_list[10], (D,), 0.5, 4.0, ((0, 2),))
    bias_out = noise(key_list[11], (D,), 0.3, 4.0, ((0, 2),))
    gain_two = jnp.clip(1.0 + 0.15 * jax.random.normal(key_list[12], (D,), jnp.float32), 0.25, 1.75).astype(jnp.bfloat16)
    shift_two = noise(key_list[13], (D,), 0.3, 4.0, ((0, 2),))
    bias_up = noise(key_list[14], (FF,), 0.5, 4.0, ((0, 2),))
    bias_down = noise(key_list[15], (D,), 0.3, 4.0, ((0, 2),))
    return dict(tokens=tokens, documents=documents, cotangent=cotangent, w_qkv=w_qkv, w_out=w_out, w_up=w_up, w_down=w_down, gain_one=gain_one, shift_one=shift_one, bias_query=bias_query, bias_value=bias_value, bias_out=bias_out, gain_two=gain_two, shift_two=shift_two, bias_up=bias_up, bias_down=bias_down)


@jax.custom_vjp
def low(v):
    return lax.optimization_barrier(v.astype(jnp.bfloat16)).astype(jnp.float32)

@jax.custom_vjp
def low_back(v):
    return v

def low_keep(v):
    return (low(v), None)

def low_pass(kept, grad):
    return (grad,)

def back_keep(v):
    return (v, None)

def back_low(kept, grad):
    return (low(grad),)
low.defvjp(low_keep, low_pass)
low_back.defvjp(back_keep, back_low)
epsilon = 1e-05

def product(former, latter):
    return jnp.dot(former, latter, precision=lax.Precision.HIGHEST)

def layer_norm(values, gain_row, shift_row):
    center = values - lax.optimization_barrier(jnp.mean(values, axis=-1, keepdims=True))
    spread = lax.optimization_barrier(jnp.mean(center * center, axis=-1, keepdims=True))
    return center * lax.rsqrt(spread + epsilon) * gain_row + shift_row

def forward(seq_tokens, doc_ids, params):
    w_qkv, w_out, w_up, w_down, gain_one, shift_one, bias_query, bias_value, bias_out, gain_two, shift_two, bias_up, bias_down = params
    length = seq_tokens.shape[0]
    normed_one = low(layer_norm(seq_tokens, gain_one, shift_one))
    project = product(normed_one, w_qkv)
    query = low(low_back(project[:, :D] + bias_query)).reshape(length, HEADS, HDIM)
    key_part = low(low_back(project[:, D:2 * D])).reshape(length, HEADS, HDIM)
    value_part = low(low_back(project[:, 2 * D:] + bias_value)).reshape(length, HEADS, HDIM)
    places = jnp.arange(length)
    allowed = (places[None, :] <= places[:, None]) & (doc_ids[None, :] == doc_ids[:, None])
    scores = low_back(jnp.einsum('qhd,khd->hqk', query, key_part, precision=lax.Precision.HIGHEST) * HDIM ** (-0.5))
    scores = jnp.where(allowed[None], scores, -1e+30)
    row_max = lax.optimization_barrier(jnp.max(scores, axis=-1, keepdims=True))
    exponent = jnp.exp(scores - row_max)
    probs = low(exponent / lax.optimization_barrier(jnp.sum(exponent, axis=-1, keepdims=True)))
    attended = jnp.einsum('hqk,khd->qhd', probs, value_part, precision=lax.Precision.HIGHEST)
    heads = low(low_back(attended.reshape(length, D)))
    branch = low_back(product(heads, w_out) + bias_out)
    middle = seq_tokens + branch
    normed_two = low(layer_norm(middle, gain_two, shift_two))
    pre_active = low_back(product(normed_two, w_up) + bias_up)
    active = low(jax.nn.gelu(pre_active, approximate=True))
    return middle + low_back(product(active, w_down) + bias_down)

def reference(tokens, documents, cotangent, w_qkv, w_out, w_up, w_down, gain_one, shift_one, bias_query, bias_value, bias_out, gain_two, shift_two, bias_up, bias_down):
    params = tuple((member.astype(jnp.float32) for member in (w_qkv, w_out, w_up, w_down, gain_one, shift_one, bias_query, bias_value, bias_out, gain_two, shift_two, bias_up, bias_down)))

    def one_sequence(totals, sequence_item):
        seq_tokens, doc_ids, seq_cotangent = sequence_item

        def run_layer(inputs, *weights):
            return forward(inputs, doc_ids, weights)
        result, pull_back = jax.vjp(run_layer, seq_tokens.astype(jnp.float32), *params)
        gradients = pull_back(seq_cotangent.astype(jnp.float32))
        totals = tuple((former + latter for former, latter in zip(totals, gradients[1:])))
        return (totals, (result.astype(jnp.bfloat16), gradients[0].astype(jnp.bfloat16)))
    zero_totals = tuple((jnp.zeros_like(member) for member in params))
    totals, (output, input_grad) = lax.scan(one_sequence, zero_totals, (tokens, documents, cotangent))
    return (output, input_grad, totals[0], totals[1], totals[2], totals[3], totals[4], totals[5], totals[6], totals[7], totals[8], totals[9], totals[10], totals[11], totals[12])
```

```python
import jax
import jax.numpy as jnp
from jax import lax
from jax.experimental import pallas as pl
from jax.experimental.pallas import tpu as pltpu
from jax.sharding import PartitionSpec as P

HDIM = 64
SCALE = HDIM ** (-0.5)
SKIP = 128
epsilon = 1e-05
bfloat = jnp.bfloat16
single = jnp.float32


def dot(former, latter, former_axis, latter_axis):
    return lax.dot_general(
        former,
        latter,
        (((former_axis,), (latter_axis,)), ((), ())),
        preferred_element_type=single,
    )


def query_chunks(length):
    early = length - SKIP
    half = length // 2
    cuts = [(0, half, 0), (half, early, 0), (early, length, early)]
    return [(a, b, first, early + b) for a, b, first in cuts]


def fill_bias(bias_ref, doc_row_ref, doc_col_ref, early_col_ref, flag_ref):
    length = doc_row_ref.shape[1]
    early = length - SKIP
    row = doc_row_ref[...]
    ok = (early_col_ref[SKIP:, :] == row) & (flag_ref[0] > 0)
    bias_ref[:early, :] = jnp.where(ok, 0.0, -1e30)
    key_at = lax.broadcasted_iota(jnp.int32, (length, length), 0)
    query_at = lax.broadcasted_iota(jnp.int32, (length, length), 1)
    ok = (doc_col_ref[...] == row) & (key_at <= query_at)
    bias_ref[early:, :] = jnp.where(ok, 0.0, -1e30)


def attend_kernel(
    flag_ref,
    doc_row_ref,
    doc_col_ref,
    early_col_ref,
    q_ref,
    k_ref,
    v_ref,
    ek_ref,
    ev_ref,
    o_ref,
    lse_ref,
    bias_ref,
    kk_ref,
    vv_ref,
):
    length = q_ref.shape[1]
    early = length - SKIP

    @pl.when(pl.program_id(0) == 0)
    def _():
        fill_bias(bias_ref, doc_row_ref, doc_col_ref, early_col_ref, flag_ref)

    kk_ref[:, :early] = ek_ref[...]
    kk_ref[:, early:] = k_ref[...]
    vv_ref[:, :early] = ev_ref[...]
    vv_ref[:, early:] = v_ref[...]
    for a, b, first, last in query_chunks(length):
        scores = dot(kk_ref[:, first:last], q_ref[:, a:b], 0, 0) * SCALE
        scores = scores + bias_ref[first:last, a:b]
        top = jnp.max(scores, axis=0, keepdims=True)
        exponent = jnp.exp(scores - top)
        norm = jnp.sum(exponent, axis=0, keepdims=True)
        out = dot(vv_ref[:, first:last], exponent.astype(bfloat), 1, 0) / norm
        o_ref[:, a:b] = out.astype(bfloat)
        lse_ref[0, :, a:b] = top + jnp.log(norm)


def attend_back_kernel(
    flag_ref,
    doc_row_ref,
    doc_col_ref,
    early_col_ref,
    q_ref,
    k_ref,
    v_ref,
    ek_ref,
    ev_ref,
    g_ref,
    o_ref,
    lse_ref,
    dq_ref,
    dk_ref,
    dv_ref,
    dek_ref,
    dev_ref,
    bias_ref,
    kk_ref,
    vv_ref,
    dkk_ref,
    dvv_ref,
):
    length = q_ref.shape[1]
    early = length - SKIP

    @pl.when(pl.program_id(0) == 0)
    def _():
        fill_bias(bias_ref, doc_row_ref, doc_col_ref, early_col_ref, flag_ref)

    kk_ref[:, :early] = ek_ref[...]
    kk_ref[:, early:] = k_ref[...]
    vv_ref[:, :early] = ev_ref[...]
    vv_ref[:, early:] = v_ref[...]
    dkk_ref[...] = jnp.zeros_like(dkk_ref)
    dvv_ref[...] = jnp.zeros_like(dvv_ref)
    for a, b, first, last in query_chunks(length):
        queries = q_ref[:, a:b]
        grads = g_ref[:, a:b]
        keys = kk_ref[:, first:last]
        values = vv_ref[:, first:last]
        inner = jnp.sum(
            grads.astype(single) * o_ref[:, a:b].astype(single), axis=0, keepdims=True
        )
        scores = dot(keys, queries, 0, 0) * SCALE + bias_ref[first:last, a:b]
        probs = jnp.exp(scores - lse_ref[0, :, a:b])
        grad_probs = dot(values, grads, 0, 0)
        grad_scores = (probs * (grad_probs - inner)).astype(bfloat)
        dvv_ref[:, first:last] += dot(grads, probs.astype(bfloat), 1, 1)
        dkk_ref[:, first:last] += dot(queries, grad_scores, 1, 1)
        dq_ref[:, a:b] = (dot(keys, grad_scores, 1, 0) * SCALE).astype(bfloat)
    dk_ref[...] = dkk_ref[:, early:] * SCALE
    dv_ref[...] = dvv_ref[:, early:]
    dek_ref[...] = (dkk_ref[:, :early] * SCALE).astype(bfloat)
    dev_ref[...] = dvv_ref[:, :early].astype(bfloat)


def attention_specs(length, heads):
    early = length - SKIP
    block = lambda skip: pl.BlockSpec((HDIM, length), lambda h: (h + skip, 0))
    early_block = lambda skip: pl.BlockSpec((HDIM, early), lambda h: (h + skip, 0))
    whole = lambda shape: pl.BlockSpec(shape, lambda h: (0, 0))
    row_block = pl.BlockSpec((1, 1, length), lambda h: (h, 0, 0))
    inputs = [
        pl.BlockSpec(memory_space=pltpu.SMEM),
        whole((1, length)),
        whole((length, 1)),
        whole((length, 1)),
        block(0),
        block(heads),
        block(2 * heads),
        early_block(0),
        early_block(heads),
    ]
    scratch = [
        pltpu.VMEM((length + early, length), single),
        pltpu.VMEM((HDIM, length + early), bfloat),
        pltpu.VMEM((HDIM, length + early), bfloat),
    ]
    return block(0), early_block(0), row_block, inputs, scratch


def attend(flag, documents, early_docs, qkv, early_kv):
    width, length = qkv.shape[0] // 3, qkv.shape[1]
    heads = width // HDIM
    block, _, row_block, inputs, scratch = attention_specs(length, heads)
    return pl.pallas_call(
        attend_kernel,
        grid=(heads,),
        in_specs=inputs,
        out_specs=[block, row_block],
        out_shape=[
            jax.ShapeDtypeStruct((width, length), bfloat),
            jax.ShapeDtypeStruct((heads, 1, length), single),
        ],
        scratch_shapes=scratch,
        compiler_params=pltpu.CompilerParams(vmem_limit_bytes=32 * 2**20),
        cost_estimate=pl.CostEstimate(
            flops=12 * 10**9, bytes_accessed=6 * 10**6, transcendentals=0
        ),
        name="attend",
    )(
        flag,
        documents.reshape(1, length),
        documents.reshape(length, 1),
        early_docs.reshape(length, 1),
        qkv,
        qkv,
        qkv,
        early_kv,
        early_kv,
    )


def attend_back(flag, documents, early_docs, qkv, early_kv, grads, outs, lse):
    width, length = qkv.shape[0] // 3, qkv.shape[1]
    heads = width // HDIM
    early = length - SKIP
    block, early_block, row_block, inputs, scratch = attention_specs(length, heads)
    return pl.pallas_call(
        attend_back_kernel,
        grid=(heads,),
        in_specs=inputs + [block, block, row_block],
        out_specs=[block, block, block, early_block, early_block],
        out_shape=[
            jax.ShapeDtypeStruct((width, length), bfloat),
            jax.ShapeDtypeStruct((width, length), single),
            jax.ShapeDtypeStruct((width, length), single),
            jax.ShapeDtypeStruct((width, early), bfloat),
            jax.ShapeDtypeStruct((width, early), bfloat),
        ],
        scratch_shapes=scratch
        + [
            pltpu.VMEM((HDIM, length + early), single),
            pltpu.VMEM((HDIM, length + early), single),
        ],
        compiler_params=pltpu.CompilerParams(vmem_limit_bytes=32 * 2**20),
        cost_estimate=pl.CostEstimate(
            flops=30 * 10**9, bytes_accessed=12 * 10**6, transcendentals=0
        ),
        name="attend_back",
    )(
        flag,
        documents.reshape(1, length),
        documents.reshape(length, 1),
        early_docs.reshape(length, 1),
        qkv,
        qkv,
        qkv,
        early_kv,
        early_kv,
        grads,
        outs,
        lse,
    )


def swapped(block):
    return lax.ppermute(block, "shard", [(0, 1), (1, 0)])


def halves(block, at):
    middle = block.shape[0] // 2
    lower, upper = block[:middle], block[middle:]
    first = at == 0
    return jnp.where(first, lower, upper), jnp.where(first, upper, lower)


def both_tokens(mine, arrived):
    return jnp.concatenate([mine, arrived], axis=1)


def partners(count, bit):
    return [(i, i ^ (1 << bit)) for i in range(count)]


def window(rows):
    return -(-rows // 16) * 8


def summed_product(former, latter, order):
    count = lax.axis_size("replica")
    at = lax.axis_index("replica")
    if not order:
        return lax.psum(dot(former, latter, 1, 1), "replica")
    sizes = []
    total = None
    for bit in order:
        source = former if total is None else total
        rows = source.shape[0]
        size = window(rows)
        low = ((at >> bit) & 1) == 0
        lower, upper = source[:size], source[rows - size :]
        sent, kept = jnp.where(low, upper, lower), jnp.where(low, lower, upper)
        if total is None:
            sent = dot(sent, latter, 1, 1)
            kept = dot(kept, latter, 1, 1)
        arrived = lax.ppermute(sent.astype(bfloat), "replica", partners(count, bit))
        total = kept + arrived.astype(single)
        sizes.append(rows)
    whole = total.astype(bfloat)
    for bit, rows in zip(order[::-1], sizes[::-1]):
        low = ((at >> bit) & 1) == 0
        arrived = lax.ppermute(whole, "replica", partners(count, bit))
        lower, upper = jnp.where(low, whole, arrived), jnp.where(low, arrived, whole)
        whole = jnp.concatenate([lower, upper[2 * window(rows) - rows :]], axis=0)
    return whole.astype(single)


def summed_small(values):
    count = lax.axis_size("replica")
    if count & (count - 1):
        return lax.psum(values, "replica")
    for bit in range(count.bit_length() - 1):
        values = values + lax.ppermute(values, "replica", partners(count, bit))
    return values


def orders():
    count = lax.axis_size("replica")
    if count & (count - 1):
        return (), ()
    bits = tuple(range(count.bit_length() - 1))
    return bits, bits[1:2] + bits[:1] + bits[2:]


def normalize(values):
    center = values - jnp.mean(values, axis=0, keepdims=True)
    spread = jnp.mean(center * center, axis=0, keepdims=True)
    scale = lax.rsqrt(spread + epsilon)
    return center * scale, scale


def normalize_back(grad, normal, scale, gain):
    z = grad * gain
    z_mean = jnp.mean(z, axis=0, keepdims=True)
    zn_mean = jnp.mean(z * normal, axis=0, keepdims=True)
    part = (z - z_mean - normal * zn_mean) * scale
    return part, jnp.sum(grad * normal, axis=1), jnp.sum(grad, axis=1)


def tanh_gelu(values):
    return jax.nn.gelu(values, approximate=True)


def shards(
    tokens,
    documents,
    cotangent,
    w_qkv,
    w_out,
    w_up,
    w_down,
    gain_one,
    shift_one,
    bias_query,
    bias_value,
    bias_out,
    gain_two,
    shift_two,
    bias_up,
    bias_down,
):
    at = lax.axis_index("shard")
    first = at == 0
    flag = at.astype(jnp.int32).reshape(1)
    order_one, order_two = orders()
    docs = documents[0]
    early_docs = lax.ppermute(docs, "shard", [(0, 1)])

    other_qkv = swapped(w_qkv)
    vectors = jnp.stack(
        [
            gain_one,
            shift_one,
            bias_query,
            bias_value,
            bias_out,
            gain_two,
            shift_two,
            bias_down,
        ]
    )
    other_vectors, other_up_bias = swapped((vectors, bias_up))
    full_out = lax.all_gather(w_out, "shard", axis=0, tiled=True)
    full_up = lax.all_gather(w_up, "shard", axis=0, tiled=True)
    full_down = lax.all_gather(w_down.T, "shard", axis=1, tiled=True)

    def ordered(mine, other, axis):
        return jnp.concatenate(
            [jnp.where(first, mine, other), jnp.where(first, other, mine)], axis=axis
        )

    columns = ordered(vectors, other_vectors, 1).T.astype(single)
    (
        col_gain_one,
        col_shift_one,
        col_query,
        col_value,
        col_out,
        col_gain_two,
        col_shift_two,
        col_down,
    ) = [columns[:, i : i + 1] for i in range(8)]
    col_up = ordered(bias_up, other_up_bias, 0).astype(single)[:, None]

    grad_rows = cotangent[0].T
    other_grad_rows = swapped(grad_rows)
    width = grad_rows.shape[0]

    rows = tokens[0].T.astype(single)
    normal_one, scale_one = normalize(rows)
    normed_one = (normal_one * col_gain_one + col_shift_one).astype(bfloat)
    normed_one_mine, normed_one_theirs = halves(normed_one, at)
    project = dot(w_qkv, normed_one_mine, 0, 0) + dot(other_qkv, normed_one_theirs, 0, 0)
    col_qkv = jnp.concatenate([col_query, jnp.zeros_like(col_query), col_value], axis=0)
    qkv = (project + col_qkv).astype(bfloat)
    early_kv = lax.ppermute(qkv[width:, SKIP:], "shard", [(0, 1)])
    normed_one_arrived = swapped(normed_one_theirs)

    heads, lse = attend(flag, docs, early_docs, qkv, early_kv)
    heads_mine, heads_theirs = halves(heads, at)
    heads_arrived = swapped(heads_theirs)
    middle = rows + dot(full_out, heads, 0, 0) + col_out
    normal_two, scale_two = normalize(middle)
    normed_two = (normal_two * col_gain_two + col_shift_two).astype(bfloat)
    normed_two_mine, normed_two_theirs = halves(normed_two, at)
    normed_two_arrived = swapped(normed_two_theirs)
    pre_active = dot(full_up, normed_two, 0, 0) + col_up
    active, gelu_pull = jax.vjp(tanh_gelu, pre_active)
    active = active.astype(bfloat)
    active_mine, active_theirs = halves(active, at)
    active_arrived = swapped(active_theirs)
    output = (middle + dot(full_down, active, 1, 0) + col_down).astype(bfloat)

    all_grad_rows = both_tokens(grad_rows, other_grad_rows)
    all_active = both_tokens(active_mine, active_arrived)
    middle_row = width // 2
    grad_w_down = jnp.concatenate(
        [
            summed_product(all_grad_rows[:middle_row], all_active, order_one),
            summed_product(all_grad_rows[middle_row:], all_active, order_two),
        ],
        axis=0,
    ).T
    grad_bias_down = jnp.sum(grad_rows.astype(single), axis=1)
    grad_active = dot(full_down, grad_rows, 0, 0)
    grad_pre = gelu_pull(grad_active)[0].astype(bfloat)
    all_grad_pre = both_tokens(grad_pre, swapped(grad_pre))
    grad_bias_up = jnp.sum(grad_pre.astype(single), axis=1)
    all_normed_two = both_tokens(normed_two_mine, normed_two_arrived)
    ff = grad_pre.shape[0]
    grad_w_up = jnp.concatenate(
        [
            summed_product(all_normed_two, all_grad_pre[: ff // 2], order_one),
            summed_product(all_normed_two, all_grad_pre[ff // 2 :], order_two),
        ],
        axis=1,
    )
    grad_normed_two = dot(full_up, grad_pre, 1, 0)
    part_two, grad_gain_two, grad_shift_two = normalize_back(
        grad_normed_two, normal_two, scale_two, col_gain_two
    )
    grad_middle = grad_rows.astype(single) + part_two
    grad_branch = grad_middle.astype(bfloat)
    grad_bias_out = jnp.sum(grad_branch.astype(single), axis=1)
    grad_w_out = summed_product(
        both_tokens(heads_mine, heads_arrived),
        both_tokens(grad_branch, swapped(grad_branch)),
        order_one,
    )
    grad_heads = dot(full_out, grad_branch, 1, 0).astype(bfloat)
    grad_query, grad_key, grad_value, early_key, early_value = attend_back(
        flag, docs, early_docs, qkv, early_kv, grad_heads, heads, lse
    )
    back_key, back_value = lax.ppermute((early_key, early_value), "shard", [(1, 0)])

    def joined(own, back):
        return (own + jnp.pad(back.astype(single), ((0, 0), (SKIP, 0)))).astype(bfloat)

    grad_value = joined(grad_value, back_value)
    grad_project = jnp.concatenate(
        [grad_query, joined(grad_key, back_key), grad_value], axis=0
    )
    grad_bias_query = jnp.sum(grad_query.astype(single), axis=1)
    grad_bias_value = jnp.sum(grad_value.astype(single), axis=1)
    all_grad_project = both_tokens(grad_project, swapped(grad_project))
    all_normed_one = both_tokens(normed_one_mine, normed_one_arrived)
    cut = (all_grad_project.shape[0] // 256 + 1) * 128
    grad_w_qkv = jnp.concatenate(
        [
            summed_product(all_normed_one, all_grad_project[:cut], order_two),
            summed_product(all_normed_one, all_grad_project[cut:], order_one),
        ],
        axis=1,
    )
    grad_normed_one = ordered(
        dot(w_qkv, grad_project, 1, 0), dot(other_qkv, grad_project, 1, 0), 0
    )
    part_one, grad_gain_one, grad_shift_one = normalize_back(
        grad_normed_one, normal_one, scale_one, col_gain_one
    )
    input_grad = (grad_middle + part_one).astype(bfloat)

    small = jnp.stack(
        [
            grad_gain_one,
            grad_shift_one,
            grad_bias_query,
            grad_bias_value,
            grad_bias_out,
            grad_gain_two,
            grad_shift_two,
            grad_bias_down,
        ]
    )
    half = width // 2
    lanes = grad_bias_up.shape[0] // 2 // half
    up_parts = grad_bias_up.reshape(2, lanes, half)
    lower = jnp.concatenate([small[:, :half], up_parts[0]], axis=0)
    upper = jnp.concatenate([small[:, half:], up_parts[1]], axis=0)
    mine, theirs = jnp.where(first, lower, upper), jnp.where(first, upper, lower)
    mine = summed_small(mine + swapped(theirs))
    return (
        output.T[None],
        input_grad.T[None],
        grad_w_qkv,
        grad_w_out,
        grad_w_up,
        grad_w_down,
        mine[0],
        mine[1],
        mine[2],
        mine[3],
        mine[4],
        mine[5],
        mine[6],
        mine[8:].reshape(-1),
        mine[7],
    )


def solution(mesh):
    sequences = P("replica", "shard", None)
    matrix = P("shard", None)
    vector = P("shard")
    return jax.shard_map(
        shards,
        mesh=mesh,
        in_specs=(sequences, P("replica", "shard"), sequences) + (matrix,) * 4 + (vector,) * 9,
        out_specs=(sequences, sequences) + (matrix,) * 4 + (vector,) * 9,
        check_vma=False,
    )
```

```python
import jax
import jax.numpy as jnp
from jax import lax
from jax.experimental import pallas as pl
from jax.experimental.pallas import tpu as pltpu
from jax.sharding import PartitionSpec as P

HDIM = 64
SCALE = HDIM ** (-0.5)
SKIP = 128
epsilon = 1e-05
bfloat = jnp.bfloat16
single = jnp.float32


def dot(former, latter, former_axis, latter_axis):
    return lax.dot_general(
        former,
        latter,
        (((former_axis,), (latter_axis,)), ((), ())),
        preferred_element_type=single,
    )


def query_chunks(length):
    early = length - SKIP
    half = length // 2
    cuts = [(0, half, 0), (half, early, 0), (early, length, early)]
    return [(a, b, first, early + b) for a, b, first in cuts]


def fill_bias(bias_ref, doc_row_ref, doc_col_ref, early_col_ref, flag_ref):
    length = doc_row_ref.shape[1]
    early = length - SKIP
    row = doc_row_ref[...]
    ok = (early_col_ref[SKIP:, :] == row) & (flag_ref[0] > 0)
    bias_ref[:early, :] = jnp.where(ok, 0.0, -1e30)
    key_at = lax.broadcasted_iota(jnp.int32, (length, length), 0)
    query_at = lax.broadcasted_iota(jnp.int32, (length, length), 1)
    ok = (doc_col_ref[...] == row) & (key_at <= query_at)
    bias_ref[early:, :] = jnp.where(ok, 0.0, -1e30)


def attend_kernel(
    flag_ref,
    doc_row_ref,
    doc_col_ref,
    early_col_ref,
    q_ref,
    k_ref,
    v_ref,
    ek_ref,
    ev_ref,
    o_ref,
    lse_ref,
    bias_ref,
    kk_ref,
    vv_ref,
):
    length = q_ref.shape[1]
    early = length - SKIP

    @pl.when(pl.program_id(0) == 0)
    def _():
        fill_bias(bias_ref, doc_row_ref, doc_col_ref, early_col_ref, flag_ref)

    kk_ref[:, :early] = ek_ref[...]
    kk_ref[:, early:] = k_ref[...]
    vv_ref[:, :early] = ev_ref[...]
    vv_ref[:, early:] = v_ref[...]
    for a, b, first, last in query_chunks(length):
        scores = dot(kk_ref[:, first:last], q_ref[:, a:b], 0, 0) * SCALE
        scores = scores + bias_ref[first:last, a:b]
        top = jnp.max(scores, axis=0, keepdims=True)
        exponent = jnp.exp(scores - top)
        norm = jnp.sum(exponent, axis=0, keepdims=True)
        out = dot(vv_ref[:, first:last], exponent.astype(bfloat), 1, 0) / norm
        o_ref[:, a:b] = out.astype(bfloat)
        lse_ref[0, :, a:b] = top + jnp.log(norm)


def attend_back_kernel(
    flag_ref,
    doc_row_ref,
    doc_col_ref,
    early_col_ref,
    q_ref,
    k_ref,
    v_ref,
    ek_ref,
    ev_ref,
    g_ref,
    o_ref,
    lse_ref,
    dq_ref,
    dk_ref,
    dv_ref,
    dek_ref,
    dev_ref,
    bias_ref,
    kk_ref,
    vv_ref,
    dkk_ref,
    dvv_ref,
):
    length = q_ref.shape[1]
    early = length - SKIP

    @pl.when(pl.program_id(0) == 0)
    def _():
        fill_bias(bias_ref, doc_row_ref, doc_col_ref, early_col_ref, flag_ref)

    kk_ref[:, :early] = ek_ref[...]
    kk_ref[:, early:] = k_ref[...]
    vv_ref[:, :early] = ev_ref[...]
    vv_ref[:, early:] = v_ref[...]
    dkk_ref[...] = jnp.zeros_like(dkk_ref)
    dvv_ref[...] = jnp.zeros_like(dvv_ref)
    for a, b, first, last in query_chunks(length):
        queries = q_ref[:, a:b]
        grads = g_ref[:, a:b]
        keys = kk_ref[:, first:last]
        values = vv_ref[:, first:last]
        inner = jnp.sum(
            grads.astype(single) * o_ref[:, a:b].astype(single), axis=0, keepdims=True
        )
        scores = dot(keys, queries, 0, 0) * SCALE + bias_ref[first:last, a:b]
        probs = jnp.exp(scores - lse_ref[0, :, a:b])
        grad_probs = dot(values, grads, 0, 0)
        grad_scores = (probs * (grad_probs - inner)).astype(bfloat)
        dvv_ref[:, first:last] += dot(grads, probs.astype(bfloat), 1, 1)
        dkk_ref[:, first:last] += dot(queries, grad_scores, 1, 1)
        dq_ref[:, a:b] = (dot(keys, grad_scores, 1, 0) * SCALE).astype(bfloat)
    dk_ref[...] = dkk_ref[:, early:] * SCALE
    dv_ref[...] = dvv_ref[:, early:]
    dek_ref[...] = (dkk_ref[:, :early] * SCALE).astype(bfloat)
    dev_ref[...] = dvv_ref[:, :early].astype(bfloat)


def attention_specs(length, heads, begin=0):
    early = length - SKIP
    block = lambda skip: pl.BlockSpec((HDIM, length), lambda h: (h + begin + skip, 0))
    early_block = lambda skip: pl.BlockSpec((HDIM, early), lambda h: (h + begin + skip, 0))
    whole = lambda shape: pl.BlockSpec(shape, lambda h: (0, 0))
    row_block = pl.BlockSpec((1, 1, length), lambda h: (h + begin, 0, 0))
    inputs = [
        pl.BlockSpec(memory_space=pltpu.SMEM),
        whole((1, length)),
        whole((length, 1)),
        whole((length, 1)),
        block(0),
        block(heads),
        block(2 * heads),
        early_block(0),
        early_block(heads),
    ]
    scratch = [
        pltpu.VMEM((length + early, length), single),
        pltpu.VMEM((HDIM, length + early), bfloat),
        pltpu.VMEM((HDIM, length + early), bfloat),
    ]
    return block(0), early_block(0), row_block, inputs, scratch


def attend(flag, documents, early_docs, qkv, early_kv):
    width, length = qkv.shape[0] // 3, qkv.shape[1]
    heads = width // HDIM
    block, _, row_block, inputs, scratch = attention_specs(length, heads)
    return pl.pallas_call(
        attend_kernel,
        grid=(heads,),
        in_specs=inputs,
        out_specs=[block, row_block],
        out_shape=[
            jax.ShapeDtypeStruct((width, length), bfloat),
            jax.ShapeDtypeStruct((heads, 1, length), single),
        ],
        scratch_shapes=scratch,
        compiler_params=pltpu.CompilerParams(vmem_limit_bytes=32 * 2**20),
        cost_estimate=pl.CostEstimate(
            flops=12 * 10**9, bytes_accessed=6 * 10**6, transcendentals=0
        ),
        name="attend",
    )(
        flag,
        documents.reshape(1, length),
        documents.reshape(length, 1),
        early_docs.reshape(length, 1),
        qkv,
        qkv,
        qkv,
        early_kv,
        early_kv,
    )


def attend_back(flag, documents, early_docs, qkv, early_kv, grads, outs, lse, begin, end):
    length = qkv.shape[1]
    early = length - SKIP
    heads = qkv.shape[0] // 3 // HDIM
    block, early_block, row_block, inputs, scratch = attention_specs(length, heads, begin)
    width = (end - begin) * HDIM
    out_block, early_block, *_ = attention_specs(length, heads)
    return pl.pallas_call(
        attend_back_kernel,
        grid=(end - begin,),
        in_specs=inputs + [block, block, row_block],
        out_specs=[out_block, out_block, out_block, early_block, early_block],
        out_shape=[
            jax.ShapeDtypeStruct((width, length), bfloat),
            jax.ShapeDtypeStruct((width, length), single),
            jax.ShapeDtypeStruct((width, length), single),
            jax.ShapeDtypeStruct((width, early), bfloat),
            jax.ShapeDtypeStruct((width, early), bfloat),
        ],
        scratch_shapes=scratch
        + [
            pltpu.VMEM((HDIM, length + early), single),
            pltpu.VMEM((HDIM, length + early), single),
        ],
        compiler_params=pltpu.CompilerParams(vmem_limit_bytes=32 * 2**20),
        cost_estimate=NO_COST,
        name="attend_back",
    )(
        flag,
        documents.reshape(1, length),
        documents.reshape(length, 1),
        early_docs.reshape(length, 1),
        qkv,
        qkv,
        qkv,
        early_kv,
        early_kv,
        grads,
        outs,
        lse,
    )


def swapped(block):
    return lax.ppermute(block, "shard", [(0, 1), (1, 0)])


def halves(block, at):
    middle = block.shape[0] // 2
    lower, upper = block[:middle], block[middle:]
    first = at == 0
    return jnp.where(first, lower, upper), jnp.where(first, upper, lower)


class Line:
    def __init__(self):
        self.standing = []

    def enter(self, *values):
        standing = tuple(holder[key] for holder, key in self.standing)
        passed = lax.optimization_barrier(values + standing)
        for (holder, key), value in zip(self.standing, passed[len(values) :]):
            holder[key] = value
        self.standing = []
        return passed[: len(values)]

    def leave(self, holder, sent=(), **values):
        passed = lax.optimization_barrier(tuple(sent) + tuple(values.values()))
        holder.update(zip(values, passed[len(sent) :]))
        self.standing += [(holder, key) for key in values]
        return passed[: len(sent)]


def window(rows):
    return -(-rows // 16) * 8


class Sum:
    def __init__(self, line, order):
        count = lax.axis_size("replica")
        bits = count.bit_length() - 1
        self.line = line
        self.plain = count != 1 << bits
        self.order = list(order) if len(order) <= bits else []
        self.order += [(i, i) for i in range(len(self.order), bits)]
        self.place = 0
        self.sizes = []

    def low(self, bit):
        at = jnp.where(lax.axis_index("shard") == 0, bit[0], bit[1])
        return ((lax.axis_index("replica") >> at) & 1) == 0

    def pass_on(self, block, bit):
        count = lax.axis_size("replica")
        route = [
            (core * count + i, core * count + (i ^ (1 << bit[core])))
            for core in range(2)
            for i in range(count)
        ]
        self.arrived = lax.ppermute(block, ("shard", "replica"), route)

    def split(self, block, bit):
        rows = block.shape[0]
        size = window(rows)
        low = self.low(bit)
        lower, upper = block[:size], block[rows - size :]
        return jnp.where(low, upper, lower), jnp.where(low, lower, upper)

    def send(self, pairs):
        if self.plain:
            self.pairs = pairs
            return pairs[0][0]
        bit = self.order[0]
        self.sizes.append(pairs[0][0].shape[0])
        sent = sum(dot(self.split(former, bit)[0], latter, 1, 1) for former, latter in pairs)
        return sent.astype(bfloat)

    def keep(self, pairs):
        bit = self.order[0]
        return sum(dot(self.split(former, bit)[1], latter, 1, 1) for former, latter in pairs)

    def finished(self):
        return self.place == (0 if self.plain else 2 * len(self.order) - 1)

    def step(self):
        if self.finished():
            return
        bits = len(self.order)
        if self.place < bits:
            arrived, total = self.line.enter(self.arrived, self.total)
            total = total + arrived.astype(single)
            if self.place == bits - 1:
                self.line.leave(self.__dict__, whole=total.astype(bfloat))
                self.pass_on(self.whole, self.order[-1])
            else:
                bit = self.order[self.place + 1]
                self.sizes.append(total.shape[0])
                sent, kept = self.split(total, bit)
                (sent,) = self.line.leave(self.__dict__, [sent.astype(bfloat)], total=kept)
                self.pass_on(sent, bit)
        else:
            arrived, whole = self.line.enter(self.arrived, self.whole)
            at = 2 * bits - 1 - self.place
            rows = self.sizes[at]
            low = self.low(self.order[at])
            lower, upper = jnp.where(low, whole, arrived), jnp.where(low, arrived, whole)
            whole = jnp.concatenate([lower, upper[2 * window(rows) - rows :]], axis=0)
            self.line.leave(self.__dict__, whole=whole)
            self.pass_on(self.whole, self.order[at - 1])
        self.place += 1


def assemble_kernel(groups, low_ref, *refs):
    out_ref = refs[-1]
    step = pl.program_id(0)
    at = 0
    for row, lanes in enumerate(groups):
        lane = 0
        for width in lanes:
            whole_ref, arrived_ref = refs[2 * at], refs[2 * at + 1]
            for half in range(2):
                for low, source in ((1 - half, whole_ref), (half, arrived_ref)):

                    @pl.when((step == 2 * row + half) & (low_ref[at] == low))
                    def _(lane=lane, width=width, source=source):
                        out_ref[:, lane : lane + width] = source[...].astype(single)

            lane += width
            at += 1


def assembled(line, groups):
    sums = [one for row in groups for one in row]
    if sums[0].plain:
        blocks = [
            [lax.psum(sum(dot(a, b, 1, 1) for a, b in one.pairs), "replica") for one in row]
            for row in groups
        ]
        return jnp.concatenate([jnp.concatenate(row, axis=1) for row in blocks], axis=0)
    blocks = line.enter(*[block for one in sums for block in (one.whole, one.arrived)])
    lows = jnp.stack([one.low(one.order[0]) for one in sums]).astype(jnp.int32)
    rows = blocks[0].shape[0]
    lanes = [[one.whole.shape[1] for one in row] for row in groups]
    out = pl.pallas_call(
        lambda *refs: assemble_kernel(lanes, *refs),
        grid=(2 * len(groups),),
        in_specs=[pl.BlockSpec(memory_space=pltpu.SMEM)]
        + [pl.BlockSpec(block.shape, lambda i: (0, 0)) for block in blocks],
        out_specs=pl.BlockSpec((rows, sum(lanes[0])), lambda i: (i, 0)),
        out_shape=jax.ShapeDtypeStruct((2 * rows * len(groups), sum(lanes[0])), single),
        compiler_params=pltpu.CompilerParams(vmem_limit_bytes=40 * 2**20),
        cost_estimate=NO_COST,
        name="assemble",
    )(lows, *blocks)
    return out


class SmallSum:
    def __init__(self, line):
        self.line = line
        self.place = 0
        count = lax.axis_size("replica")
        self.plain = count & (count - 1) != 0
        self.steps = 1 if self.plain else count.bit_length()

    def send(self, mine, theirs):
        (theirs,) = self.line.leave(self.__dict__, [theirs], total=mine)
        self.arrived = swapped(theirs)

    def finished(self):
        return self.place == self.steps

    def step(self):
        if self.finished():
            return
        count = lax.axis_size("replica")
        total, arrived = self.line.enter(self.total, self.arrived)
        self.line.leave(self.__dict__, total=total + arrived)
        if self.plain:
            self.total = lax.psum(self.total, "replica")
        elif self.place < self.steps - 1:
            route = [(i, i ^ (1 << self.place)) for i in range(count)]
            self.arrived = lax.ppermute(self.total, "replica", route)
        self.place += 1


NO_COST = pl.CostEstimate(flops=0, bytes_accessed=0, transcendentals=0)


def gelu_slope(values):
    root = (2 / 3.141592653589793) ** 0.5
    square = values * values
    curve = jnp.tanh(root * values * (1.0 + 0.044715 * square))
    return 0.5 * (1.0 + curve) + 0.5 * root * values * (1.0 - curve * curve) * (
        1.0 + 3 * 0.044715 * square
    )


def grad_pre_kernel(w_ref, cot_ref, pre_ref, out_ref, sum_ref):
    grad = dot(w_ref[...], cot_ref[...], 0, 0)
    grad = (grad * gelu_slope(pre_ref[...])).astype(bfloat)
    out_ref[...] = grad
    sum_ref[...] = jnp.sum(grad.astype(single), axis=1, keepdims=True)


def grad_pre_of(full_down, cotangent, pre_active):
    width, ff = full_down.shape
    length = cotangent.shape[1]
    tile = 256
    return pl.pallas_call(
        grad_pre_kernel,
        grid=(ff // tile,),
        in_specs=[
            pl.BlockSpec((width, tile), lambda i: (0, i)),
            pl.BlockSpec((width, length), lambda i: (0, 0)),
            pl.BlockSpec((tile, length), lambda i: (i, 0)),
        ],
        out_specs=[
            pl.BlockSpec((tile, length), lambda i: (i, 0)),
            pl.BlockSpec((tile, 1), lambda i: (i, 0)),
        ],
        out_shape=[
            jax.ShapeDtypeStruct((ff, length), bfloat),
            jax.ShapeDtypeStruct((ff, 1), single),
        ],
        compiler_params=pltpu.CompilerParams(vmem_limit_bytes=24 * 2**20),
        cost_estimate=NO_COST,
        name="grad_pre",
    )(full_down, cotangent, pre_active)


def grad_middle_kernel(
    w_ref, grad_ref, normal_ref, scale_ref, gain_ref, cot_ref,
    middle_ref, branch_ref, gain_sum_ref, shift_sum_ref, branch_sum_ref, total_ref,
):
    step = pl.program_id(0)
    tile = w_ref.shape[0]
    place = pl.ds(pl.multiple_of(step * tile, tile), tile)
    total_ref[place, :] = dot(w_ref[...], grad_ref[...], 1, 0)

    @pl.when(step == pl.num_programs(0) - 1)
    def _():
        width, length = total_ref.shape
        rows = width // 4
        z_sum = jnp.zeros((1, length), single)
        zn_sum = jnp.zeros((1, length), single)
        for start in range(0, width, rows):
            at = slice(start, start + rows)
            grad = total_ref[at]
            normal = normal_ref[at]
            product = grad * normal
            gain = gain_ref[at]
            gain_sum_ref[at] = jnp.sum(product, axis=1, keepdims=True)
            shift_sum_ref[at] = jnp.sum(grad, axis=1, keepdims=True)
            z_sum += jnp.sum(grad * gain, axis=0, keepdims=True)
            zn_sum += jnp.sum(product * gain, axis=0, keepdims=True)
        z_mean = z_sum / width
        zn_mean = zn_sum / width
        for start in range(0, width, rows):
            at = slice(start, start + rows)
            z = total_ref[at] * gain_ref[at]
            middle = cot_ref[at].astype(single) + (
                z - z_mean - normal_ref[at] * zn_mean
            ) * scale_ref[...]
            branch = middle.astype(bfloat)
            middle_ref[at] = middle
            branch_ref[at] = branch
            branch_sum_ref[at] = jnp.sum(branch.astype(single), axis=1, keepdims=True)


def grad_middle_of(full_up, grad_pre, normal, scale, gain, cotangent):
    width, ff = full_up.shape
    length = cotangent.shape[1]
    tile = width // 4
    whole = lambda rows, lanes: pl.BlockSpec((rows, lanes), lambda i: (0, 0))
    return pl.pallas_call(
        grad_middle_kernel,
        grid=(width // tile,),
        in_specs=[
            pl.BlockSpec((tile, ff), lambda i: (i, 0)),
            whole(ff, length),
            whole(width, length),
            whole(1, length),
            whole(width, 1),
            whole(width, length),
        ],
        out_specs=[whole(width, length), whole(width, length)] + [whole(width, 1)] * 3,
        out_shape=[
            jax.ShapeDtypeStruct((width, length), single),
            jax.ShapeDtypeStruct((width, length), bfloat),
        ]
        + [jax.ShapeDtypeStruct((width, 1), single)] * 3,
        scratch_shapes=[pltpu.VMEM((width, length), single)],
        compiler_params=pltpu.CompilerParams(vmem_limit_bytes=40 * 2**20),
        cost_estimate=NO_COST,
        name="grad_middle",
    )(full_up, grad_pre, normal, scale, gain, cotangent)


ORDER = (
    "out", "Dsend", "Dkeep", "gact", "gn2", "DA", "Usend", "Ukeep", "DA", "gheads", "Osend",
    "Okeep", "abackA", "DA", "OA", "abackB", "UA", "OA", "DA", "joinA", "joinB", "gproj",
    "OA", "gn1", "UA", "DA", "OA", "Qsend", "Qkeep", "OA", "smalls", "S", "UA", "S", "DA",
    "QA", "S", "OA", "S", "UA", "S", "OA", "QA", "DA", "UA", "OA", "QA", "UA", "DA", "QA",
    "UA", "QA", "QA", "UA", "QA", "QA",
)

ROUTES = {
    "DA": ((0, 1), (1, 0), (2, 2), (3, 3)),
    "UA": ((1, 0), (0, 1), (2, 2), (3, 3)),
    "OA": ((1, 0), (0, 1), (2, 2), (3, 3)),
    "QA": ((1, 0), (0, 1), (2, 2), (3, 3)),
}

CUTS = {
    "DA": ((0, 1088), (0, 2176)),
    "UA": ((0, 544), (0, 4352)),
    "OA": ((0, 544), (0, 1088)),
    "QA": ((0, 544), (0, 3264)),
}

LAYOUTS = {
    "D": [['DA']],
    "U": [['UA']],
    "O": [['OA']],
    "Q": [['QA']],
}


def normalize(values):
    center = values - jnp.mean(values, axis=0, keepdims=True)
    spread = jnp.mean(center * center, axis=0, keepdims=True)
    scale = lax.rsqrt(spread + epsilon)
    return center * scale, scale


def normalize_back(grad, normal, scale, gain):
    z = grad * gain
    z_mean = jnp.mean(z, axis=0, keepdims=True)
    zn_mean = jnp.mean(z * normal, axis=0, keepdims=True)
    part = (z - z_mean - normal * zn_mean) * scale
    return part, jnp.sum(grad * normal, axis=1), jnp.sum(grad, axis=1)


def tanh_gelu(values):
    return jax.nn.gelu(values, approximate=True)


def shards(
    tokens,
    documents,
    cotangent,
    w_qkv,
    w_out,
    w_up,
    w_down,
    gain_one,
    shift_one,
    bias_query,
    bias_value,
    bias_out,
    gain_two,
    shift_two,
    bias_up,
    bias_down,
):
    at = lax.axis_index("shard")
    first = at == 0
    flag = at.astype(jnp.int32).reshape(1)
    docs = documents[0]
    early_docs = lax.ppermute(docs, "shard", [(0, 1)])

    other_qkv = swapped(w_qkv)
    vectors = jnp.stack(
        [
            gain_one,
            shift_one,
            bias_query,
            bias_value,
            bias_out,
            gain_two,
            shift_two,
            bias_down,
        ]
    )
    other_vectors, other_up_bias = swapped((vectors, bias_up))
    full_out = lax.all_gather(w_out, "shard", axis=0, tiled=True)
    full_up = lax.all_gather(w_up, "shard", axis=0, tiled=True)
    full_down = lax.all_gather(w_down.T, "shard", axis=1, tiled=True)

    def ordered(mine, other, axis):
        return jnp.concatenate(
            [jnp.where(first, mine, other), jnp.where(first, other, mine)], axis=axis
        )

    columns = ordered(vectors, other_vectors, 1).T.astype(single)
    (
        col_gain_one,
        col_shift_one,
        col_query,
        col_value,
        col_out,
        col_gain_two,
        col_shift_two,
        col_down,
    ) = [columns[:, i : i + 1] for i in range(8)]
    col_up = ordered(bias_up, other_up_bias, 0).astype(single)[:, None]

    grad_rows = cotangent[0].T
    other_grad_rows = swapped(grad_rows)
    width = grad_rows.shape[0]

    rows = tokens[0].T.astype(single)
    normal_one, scale_one = normalize(rows)
    normed_one = (normal_one * col_gain_one + col_shift_one).astype(bfloat)
    normed_one_mine, normed_one_theirs = halves(normed_one, at)
    project = dot(w_qkv, normed_one_mine, 0, 0) + dot(other_qkv, normed_one_theirs, 0, 0)
    col_qkv = jnp.concatenate([col_query, jnp.zeros_like(col_query), col_value], axis=0)
    qkv = (project + col_qkv).astype(bfloat)
    early_kv = lax.ppermute(qkv[width:, SKIP:], "shard", [(0, 1)])
    normed_one_arrived = swapped(normed_one_theirs)

    qkv, early_kv, early_docs, normed_one_arrived, other_grad_rows = lax.optimization_barrier(
        (qkv, early_kv, early_docs, normed_one_arrived, other_grad_rows)
    )
    heads, lse = attend(flag, docs, early_docs, qkv, early_kv)
    heads_mine, heads_theirs = halves(heads, at)
    heads_arrived = swapped(heads_theirs)
    middle = rows + dot(full_out, heads, 0, 0) + col_out
    normal_two, scale_two = normalize(middle)
    normed_two = (normal_two * col_gain_two + col_shift_two).astype(bfloat)
    normed_two_mine, normed_two_theirs = halves(normed_two, at)
    normed_two_arrived = swapped(normed_two_theirs)
    normed_two, heads_arrived = lax.optimization_barrier((normed_two, heads_arrived))
    pre_active = dot(full_up, normed_two, 0, 0) + col_up
    active = tanh_gelu(pre_active).astype(bfloat)
    active_mine, active_theirs = halves(active, at)
    active_arrived = swapped(active_theirs)
    line = Line()
    sums = {name: Sum(line, order) for name, order in ROUTES.items()}
    sums["S"] = SmallSum(line)
    s = {}
    half = width // 2
    ff = pre_active.shape[0]

    def stage_out():
        active_now, middle_now = line.enter(active, middle)
        out = (middle_now + dot(full_down, active_now, 1, 0) + col_down).astype(bfloat)
        line.leave(s, output=out)

    def send_matrix(matrix, pairs):
        names = [name for row in LAYOUTS[matrix] for name in row]
        sent = []
        for name in names:
            rows, lanes = [slice(*at) for at in CUTS[name]]
            sent.append(
                sums[name].send([(former[rows], latter[lanes]) for former, latter in pairs])
            )
        formers, latters = zip(*pairs)
        sent = line.leave(
            s, sent, **{matrix + str(i): one for i, one in enumerate(formers + latters)}
        )
        for name, value in zip(names, sent):
            if not sums[name].plain:
                sums[name].pass_on(value, sums[name].order[0])

    def keep(matrix):
        names = [name for row in LAYOUTS[matrix] for name in row]
        if sums[names[0]].plain:
            return
        count = 2
        values = line.enter(*[s[matrix + str(i)] for i in range(2 * count)])
        for name in names:
            rows, lanes = [slice(*at) for at in CUTS[name]]
            pairs = [(a[rows], b[lanes]) for a, b in zip(values[:count], values[count:])]
            line.leave(sums[name].__dict__, total=sums[name].keep(pairs))

    def stage_down_send():
        mine, arrived, s["normed_two_arrived"], own, other = line.enter(
            active_mine, active_arrived, normed_two_arrived, grad_rows, other_grad_rows
        )
        send_matrix("D", [(own, mine), (other, arrived)])

    def stage_grad_active():
        (cot,) = line.enter(grad_rows)
        grad_pre, bias_sum = grad_pre_of(full_down, cot, pre_active)
        line.leave(s, grad_pre=grad_pre, grad_bias_up=bias_sum)
        s["grad_pre_other"] = swapped(s["grad_pre"])

    def stage_normed_two():
        (grad_pre,) = line.enter(s["grad_pre"])
        names = "grad_middle", "grad_branch", "grad_gain_two", "grad_shift_two", "grad_bias_out"
        results = grad_middle_of(
            full_up, grad_pre, normal_two, scale_two, col_gain_two, grad_rows
        )
        line.leave(s, **dict(zip(names, results)))
        s["grad_branch_other"] = swapped(s["grad_branch"])

    def stage_up_send():
        mine, arrived, own, other = line.enter(
            normed_two_mine, s["normed_two_arrived"], s["grad_pre"], s["grad_pre_other"]
        )
        send_matrix("U", [(mine, own), (arrived, other)])

    def stage_out_send():
        mine, arrived, own, other = line.enter(
            heads_mine, heads_arrived, s["grad_branch"], s["grad_branch_other"]
        )
        send_matrix("O", [(mine, own), (arrived, other)])

    def stage_grad_heads():
        grad_branch, s["grad_branch_other"] = line.enter(s["grad_branch"], s["grad_branch_other"])
        line.leave(s, grad_heads=dot(full_out, grad_branch, 1, 0).astype(bfloat))

    heads_count = width // HDIM
    ranges = {"A": (0, heads_count // 2), "B": (heads_count // 2, heads_count)}

    def stage_attend_back(name):
        (grad_heads,) = line.enter(s["grad_heads"])
        results = attend_back(
            flag, docs, early_docs, qkv, early_kv, grad_heads, heads, lse, *ranges[name]
        )
        back = jnp.concatenate(results[3:], axis=0)
        kept = {name + str(i): one for i, one in enumerate(results[:3])}
        (back,) = line.leave(s, [back], **kept)
        s["back" + name] = lax.ppermute(back, "shard", [(1, 0)])

    def joined(own, back):
        return (own + jnp.pad(back.astype(single), ((0, 0), (SKIP, 0)))).astype(bfloat)

    def stage_join(name):
        query, key, value, back = line.enter(*[s[name + str(i)] for i in range(3)], s["back" + name])
        middle_row = back.shape[0] // 2
        key, value = joined(key, back[:middle_row]), joined(value, back[middle_row:])
        line.leave(s, **{name + "q": query, name + "k": key, name + "v": value})

    def stage_project():
        pieces = line.enter(*[s[name + part] for part in "qkv" for name in "AB"])
        line.leave(s, grad_project=jnp.concatenate(pieces, axis=0))
        s["grad_project_other"] = swapped(s["grad_project"])

    def stage_normed_one():
        (grad_project,) = line.enter(s["grad_project"])
        grad_normed_one = ordered(
            dot(w_qkv, grad_project, 1, 0), dot(other_qkv, grad_project, 1, 0), 0
        )
        part_one, gain_sum, shift_sum = normalize_back(
            grad_normed_one, normal_one, scale_one, col_gain_one
        )
        line.leave(
            s,
            input_grad=(s["grad_middle"] + part_one).astype(bfloat),
            grad_gain_one=gain_sum,
            grad_shift_one=shift_sum,
        )

    def stage_small():
        bias_out, gain_two_sum, shift_two_sum, bias_up_sum, cot, grad_project = line.enter(
            s["grad_bias_out"],
            s["grad_gain_two"],
            s["grad_shift_two"],
            s["grad_bias_up"],
            grad_rows,
            s["grad_project"],
        )
        small = jnp.stack(
            [
                s["grad_gain_one"],
                s["grad_shift_one"],
                jnp.sum(grad_project[:width].astype(single), axis=1),
                jnp.sum(grad_project[2 * width :].astype(single), axis=1),
                bias_out[:, 0],
                gain_two_sum[:, 0],
                shift_two_sum[:, 0],
                jnp.sum(cot.astype(single), axis=1),
            ]
        )
        lanes = ff // 2 // half
        up_parts = bias_up_sum[:, 0].reshape(2, lanes, half)
        lower = jnp.concatenate([small[:, :half], up_parts[0]], axis=0)
        upper = jnp.concatenate([small[:, half:], up_parts[1]], axis=0)
        sums["S"].send(jnp.where(first, lower, upper), jnp.where(first, upper, lower))

    def stage_qkv_send():
        mine, arrived, own, other = line.enter(
            normed_one_mine, normed_one_arrived, s["grad_project"], s["grad_project_other"]
        )
        send_matrix("Q", [(mine, own), (arrived, other)])

    stages = {
        "out": stage_out,
        "Dsend": stage_down_send,
        "Dkeep": lambda: keep("D"),
        "gact": stage_grad_active,
        "gn2": stage_normed_two,
        "Usend": stage_up_send,
        "Ukeep": lambda: keep("U"),
        "Osend": stage_out_send,
        "Okeep": lambda: keep("O"),
        "gheads": stage_grad_heads,
        "abackA": lambda: stage_attend_back("A"),
        "abackB": lambda: stage_attend_back("B"),
        "joinA": lambda: stage_join("A"),
        "joinB": lambda: stage_join("B"),
        "gproj": stage_project,
        "gn1": stage_normed_one,
        "smalls": stage_small,
        "Qsend": stage_qkv_send,
        "Qkeep": lambda: keep("Q"),
    }
    grads = {}

    def gather():
        for name, layout in LAYOUTS.items():
            rows_of = [[sums[one] for one in row] for row in layout]
            sent = not waiting or not rows_of[0][0].plain
            if name not in grads and sent and all(
                one.finished() for row in rows_of for one in row
            ):
                grads[name] = assembled(line, rows_of)

    waiting = set(stages)
    for name in ORDER:
        if name in stages:
            stages[name]()
            waiting.remove(name)
        else:
            sums[name].step()
        if name not in stages:
            gather()
    while len(grads) < len(LAYOUTS) or not sums["S"].finished():
        for one in sums.values():
            one.step()
        gather()
    small = sums["S"].total
    return (
        s["output"].T[None],
        s["input_grad"].T[None],
        grads["Q"],
        grads["O"],
        grads["U"],
        grads["D"].T,
        small[0],
        small[1],
        small[2],
        small[3],
        small[4],
        small[5],
        small[6],
        small[8:].reshape(-1),
        small[7],
    )


def solution(mesh):
    sequences = P("replica", "shard", None)
    matrix = P("shard", None)
    vector = P("shard")
    return jax.shard_map(
        shards,
        mesh=mesh,
        in_specs=(sequences, P("replica", "shard"), sequences) + (matrix,) * 4 + (vector,) * 9,
        out_specs=(sequences, sequences) + (matrix,) * 4 + (vector,) * 9,
        check_vma=False,
    )
```

```python
import functools

import jax
import jax.numpy as jnp
from jax import lax
from jax.experimental import pallas as pl
from jax.experimental.pallas import tpu as pltpu
from jax.sharding import PartitionSpec as P

HDIM = 64
SCALE = HDIM ** (-0.5)
SKIP = 128
epsilon = 1e-05
bfloat = jnp.bfloat16
single = jnp.float32


def dot(former, latter, former_axis, latter_axis):
    return lax.dot_general(
        former,
        latter,
        (((former_axis,), (latter_axis,)), ((), ())),
        preferred_element_type=single,
    )


def query_chunks(length):
    early = length - SKIP
    half = length // 2
    cuts = [(0, half, 0), (half, early, 0), (early, length, early)]
    return [(a, b, first, early + b) for a, b, first in cuts]


def fill_bias(bias_ref, doc_row_ref, doc_col_ref, early_col_ref, flag_ref):
    length = doc_row_ref.shape[1]
    early = length - SKIP
    row = doc_row_ref[...]
    ok = (early_col_ref[SKIP:, :] == row) & (flag_ref[0] > 0)
    bias_ref[:early, :] = jnp.where(ok, 0.0, -1e30)
    key_at = lax.broadcasted_iota(jnp.int32, (length, length), 0)
    query_at = lax.broadcasted_iota(jnp.int32, (length, length), 1)
    ok = (doc_col_ref[...] == row) & (key_at <= query_at)
    bias_ref[early:, :] = jnp.where(ok, 0.0, -1e30)


def attend_kernel(
    flag_ref,
    doc_row_ref,
    doc_col_ref,
    early_col_ref,
    q_ref,
    k_ref,
    v_ref,
    ek_ref,
    ev_ref,
    o_ref,
    lse_ref,
    bias_ref,
    kk_ref,
    vv_ref,
):
    length = q_ref.shape[1]
    early = length - SKIP

    @pl.when(pl.program_id(0) == 0)
    def _():
        fill_bias(bias_ref, doc_row_ref, doc_col_ref, early_col_ref, flag_ref)

    kk_ref[:, :early] = ek_ref[...]
    kk_ref[:, early:] = k_ref[...]
    vv_ref[:, :early] = ev_ref[...]
    vv_ref[:, early:] = v_ref[...]
    for a, b, first, last in query_chunks(length):
        scores = dot(kk_ref[:, first:last], q_ref[:, a:b], 0, 0) * SCALE
        scores = scores + bias_ref[first:last, a:b]
        top = jnp.max(scores, axis=0, keepdims=True)
        exponent = jnp.exp(scores - top)
        norm = jnp.sum(exponent, axis=0, keepdims=True)
        out = dot(vv_ref[:, first:last], exponent.astype(bfloat), 1, 0) / norm
        o_ref[:, a:b] = out.astype(bfloat)
        lse_ref[0, :, a:b] = top + jnp.log(norm)


def attend_back_kernel(
    flag_ref,
    doc_row_ref,
    doc_col_ref,
    early_col_ref,
    q_ref,
    k_ref,
    v_ref,
    ek_ref,
    ev_ref,
    g_ref,
    o_ref,
    lse_ref,
    dq_ref,
    dk_ref,
    dv_ref,
    dek_ref,
    dev_ref,
    bias_ref,
    kk_ref,
    vv_ref,
    dkk_ref,
    dvv_ref,
):
    length = q_ref.shape[1]
    early = length - SKIP

    @pl.when(pl.program_id(0) == 0)
    def _():
        fill_bias(bias_ref, doc_row_ref, doc_col_ref, early_col_ref, flag_ref)

    kk_ref[:, :early] = ek_ref[...]
    kk_ref[:, early:] = k_ref[...]
    vv_ref[:, :early] = ev_ref[...]
    vv_ref[:, early:] = v_ref[...]
    dkk_ref[...] = jnp.zeros_like(dkk_ref)
    dvv_ref[...] = jnp.zeros_like(dvv_ref)
    for a, b, first, last in query_chunks(length):
        queries = q_ref[:, a:b]
        grads = g_ref[:, a:b]
        keys = kk_ref[:, first:last]
        values = vv_ref[:, first:last]
        inner = jnp.sum(
            grads.astype(single) * o_ref[:, a:b].astype(single), axis=0, keepdims=True
        )
        scores = dot(keys, queries, 0, 0) * SCALE + bias_ref[first:last, a:b]
        probs = jnp.exp(scores - lse_ref[0, :, a:b])
        grad_probs = dot(values, grads, 0, 0)
        grad_scores = (probs * (grad_probs - inner)).astype(bfloat)
        dvv_ref[:, first:last] += dot(grads, probs.astype(bfloat), 1, 1)
        dkk_ref[:, first:last] += dot(queries, grad_scores, 1, 1)
        dq_ref[:, a:b] = (dot(keys, grad_scores, 1, 0) * SCALE).astype(bfloat)
    dk_ref[...] = dkk_ref[:, early:] * SCALE
    dv_ref[...] = dvv_ref[:, early:]
    dek_ref[...] = (dkk_ref[:, :early] * SCALE).astype(bfloat)
    dev_ref[...] = dvv_ref[:, :early].astype(bfloat)


def attention_specs(length, heads, begin=0):
    early = length - SKIP
    block = lambda skip: pl.BlockSpec((HDIM, length), lambda h: (h + begin + skip, 0))
    early_block = lambda skip: pl.BlockSpec((HDIM, early), lambda h: (h + begin + skip, 0))
    whole = lambda shape: pl.BlockSpec(shape, lambda h: (0, 0))
    row_block = pl.BlockSpec((1, 1, length), lambda h: (h + begin, 0, 0))
    inputs = [
        pl.BlockSpec(memory_space=pltpu.SMEM),
        whole((1, length)),
        whole((length, 1)),
        whole((length, 1)),
        block(0),
        block(heads),
        block(2 * heads),
        early_block(0),
        early_block(heads),
    ]
    scratch = [
        pltpu.VMEM((length + early, length), single),
        pltpu.VMEM((HDIM, length + early), bfloat),
        pltpu.VMEM((HDIM, length + early), bfloat),
    ]
    return block(0), early_block(0), row_block, inputs, scratch


def attend(flag, documents, early_docs, qkv, early_kv):
    width, length = qkv.shape[0] // 3, qkv.shape[1]
    heads = width // HDIM
    block, _, row_block, inputs, scratch = attention_specs(length, heads)
    return pl.pallas_call(
        attend_kernel,
        grid=(heads,),
        in_specs=inputs,
        out_specs=[block, row_block],
        out_shape=[
            jax.ShapeDtypeStruct((width, length), bfloat),
            jax.ShapeDtypeStruct((heads, 1, length), single),
        ],
        scratch_shapes=scratch,
        compiler_params=pltpu.CompilerParams(vmem_limit_bytes=32 * 2**20),
        cost_estimate=pl.CostEstimate(
            flops=12 * 10**9, bytes_accessed=6 * 10**6, transcendentals=0
        ),
        name="attend",
    )(
        flag,
        documents.reshape(1, length),
        documents.reshape(length, 1),
        early_docs.reshape(length, 1),
        qkv,
        qkv,
        qkv,
        early_kv,
        early_kv,
    )


def attend_back(flag, documents, early_docs, qkv, early_kv, grads, outs, lse, begin, end):
    length = qkv.shape[1]
    early = length - SKIP
    heads = qkv.shape[0] // 3 // HDIM
    block, early_block, row_block, inputs, scratch = attention_specs(length, heads, begin)
    width = (end - begin) * HDIM
    out_block, early_block, *_ = attention_specs(length, heads)
    return pl.pallas_call(
        attend_back_kernel,
        grid=(end - begin,),
        in_specs=inputs + [block, block, row_block],
        out_specs=[out_block, out_block, out_block, early_block, early_block],
        out_shape=[
            jax.ShapeDtypeStruct((width, length), bfloat),
            jax.ShapeDtypeStruct((width, length), single),
            jax.ShapeDtypeStruct((width, length), single),
            jax.ShapeDtypeStruct((width, early), bfloat),
            jax.ShapeDtypeStruct((width, early), bfloat),
        ],
        scratch_shapes=scratch
        + [
            pltpu.VMEM((HDIM, length + early), single),
            pltpu.VMEM((HDIM, length + early), single),
        ],
        compiler_params=pltpu.CompilerParams(vmem_limit_bytes=32 * 2**20),
        cost_estimate=NO_COST,
        name="attend_back",
    )(
        flag,
        documents.reshape(1, length),
        documents.reshape(length, 1),
        early_docs.reshape(length, 1),
        qkv,
        qkv,
        qkv,
        early_kv,
        early_kv,
        grads,
        outs,
        lse,
    )


def swapped(block):
    return lax.ppermute(block, "shard", [(0, 1), (1, 0)])


def halves(block, at):
    middle = block.shape[0] // 2
    lower, upper = block[:middle], block[middle:]
    first = at == 0
    return jnp.where(first, lower, upper), jnp.where(first, upper, lower)


class State:
    pass


class Line:
    def __init__(self):
        self.standing = []

    def enter(self, *values):
        standing = tuple(holder[key] for holder, key in self.standing)
        passed = lax.optimization_barrier(values + standing)
        for (holder, key), value in zip(self.standing, passed[len(values) :]):
            holder[key] = value
        self.standing = []
        return passed[: len(values)]

    def leave(self, holder, sent=(), **values):
        passed = lax.optimization_barrier(tuple(sent) + tuple(values.values()))
        holder.update(zip(values, passed[len(sent) :]))
        self.standing += [(holder, key) for key in values]
        return passed[: len(sent)]


def window(rows):
    return -(-rows // 16) * 8


class Sum:
    def __init__(self, line, order):
        count = lax.axis_size("replica")
        bits = count.bit_length() - 1
        self.line = line
        self.plain = count != 1 << bits
        self.order = list(order) if len(order) <= bits else []
        self.order += [(i, i) for i in range(len(self.order), bits)]
        self.place = 0
        self.sizes = []

    def low(self, bit):
        at = jnp.where(lax.axis_index("shard") == 0, bit[0], bit[1])
        return ((lax.axis_index("replica") >> at) & 1) == 0

    def pass_on(self, block, bit):
        count = lax.axis_size("replica")
        route = [
            (core * count + i, core * count + (i ^ (1 << bit[core])))
            for core in range(2)
            for i in range(count)
        ]
        self.arrived = lax.ppermute(block, ("shard", "replica"), route)

    def split(self, block, bit):
        rows = block.shape[0]
        size = window(rows)
        low = self.low(bit)
        lower, upper = block[:size], block[rows - size :]
        return jnp.where(low, upper, lower), jnp.where(low, lower, upper)

    def send(self, pairs):
        if self.plain:
            self.pairs = pairs
            return pairs[0][0]
        bit = self.order[0]
        self.sizes.append(pairs[0][0].shape[0])
        sent = sum(dot(self.split(former, bit)[0], latter, 1, 1) for former, latter in pairs)
        return sent.astype(bfloat)

    def keep(self, pairs):
        bit = self.order[0]
        return sum(dot(self.split(former, bit)[1], latter, 1, 1) for former, latter in pairs)

    def finished(self):
        return self.place == (0 if self.plain else 2 * len(self.order) - 1)

    def step(self):
        if self.finished():
            return
        bits = len(self.order)
        if self.place < bits:
            arrived, total = self.line.enter(self.arrived, self.total)
            total = total + arrived.astype(single)
            if self.place == bits - 1:
                self.line.leave(self.__dict__, whole=total.astype(bfloat))
                self.pass_on(self.whole, self.order[-1])
            else:
                bit = self.order[self.place + 1]
                self.sizes.append(total.shape[0])
                sent, kept = self.split(total, bit)
                (sent,) = self.line.leave(self.__dict__, [sent.astype(bfloat)], total=kept)
                self.pass_on(sent, bit)
        else:
            arrived, whole = self.line.enter(self.arrived, self.whole)
            at = 2 * bits - 1 - self.place
            rows = self.sizes[at]
            low = self.low(self.order[at])
            lower, upper = jnp.where(low, whole, arrived), jnp.where(low, arrived, whole)
            whole = jnp.concatenate([lower, upper[2 * window(rows) - rows :]], axis=0)
            self.line.leave(self.__dict__, whole=whole)
            self.pass_on(self.whole, self.order[at - 1])
        self.place += 1


def assemble_kernel(groups, low_ref, *refs):
    out_ref = refs[-1]
    step = pl.program_id(0)
    at = 0
    for row, lanes in enumerate(groups):
        lane = 0
        for width in lanes:
            whole_ref, arrived_ref = refs[2 * at], refs[2 * at + 1]
            for half in range(2):
                for low, source in ((1 - half, whole_ref), (half, arrived_ref)):

                    @pl.when((step == 2 * row + half) & (low_ref[at] == low))
                    def _(lane=lane, width=width, source=source):
                        out_ref[:, lane : lane + width] = source[...].astype(single)

            lane += width
            at += 1


def assembled(line, groups):
    sums = [one for row in groups for one in row]
    if sums[0].plain:
        blocks = [
            [lax.psum(sum(dot(a, b, 1, 1) for a, b in one.pairs), "replica") for one in row]
            for row in groups
        ]
        return jnp.concatenate([jnp.concatenate(row, axis=1) for row in blocks], axis=0)
    blocks = line.enter(*[block for one in sums for block in (one.whole, one.arrived)])
    lows = jnp.stack([one.low(one.order[0]) for one in sums]).astype(jnp.int32)
    rows = blocks[0].shape[0]
    lanes = [[one.whole.shape[1] for one in row] for row in groups]
    out = pl.pallas_call(
        lambda *refs: assemble_kernel(lanes, *refs),
        grid=(2 * len(groups),),
        in_specs=[pl.BlockSpec(memory_space=pltpu.SMEM)]
        + [pl.BlockSpec(block.shape, lambda i: (0, 0)) for block in blocks],
        out_specs=pl.BlockSpec((rows, sum(lanes[0])), lambda i: (i, 0)),
        out_shape=jax.ShapeDtypeStruct((2 * rows * len(groups), sum(lanes[0])), single),
        compiler_params=pltpu.CompilerParams(vmem_limit_bytes=56 * 2**20),
        cost_estimate=NO_COST,
        name="assemble",
    )(lows, *blocks)
    return out


class SmallSum:
    def __init__(self, line):
        self.line = line
        self.place = 0
        count = lax.axis_size("replica")
        self.plain = count & (count - 1) != 0
        self.steps = 1 if self.plain else count.bit_length()

    def send(self, mine, theirs):
        (theirs,) = self.line.leave(self.__dict__, [theirs], total=mine)
        self.arrived = swapped(theirs)

    def finished(self):
        return self.place == self.steps

    def step(self):
        if self.finished():
            return
        count = lax.axis_size("replica")
        total, arrived = self.line.enter(self.total, self.arrived)
        self.line.leave(self.__dict__, total=total + arrived)
        if self.plain:
            self.total = lax.psum(self.total, "replica")
        elif self.place < self.steps - 1:
            route = [(i, i ^ (1 << self.place)) for i in range(count)]
            self.arrived = lax.ppermute(self.total, "replica", route)
        self.place += 1


NO_COST = pl.CostEstimate(flops=0, bytes_accessed=0, transcendentals=0)


def gelu_slope(values):
    root = (2 / 3.141592653589793) ** 0.5
    square = values * values
    curve = jnp.tanh(root * values * (1.0 + 0.044715 * square))
    return 0.5 * (1.0 + curve) + 0.5 * root * values * (1.0 - curve * curve) * (
        1.0 + 3 * 0.044715 * square
    )


def grad_pre_kernel(w_ref, cot_ref, pre_ref, out_ref, sum_ref):
    grad = dot(w_ref[...], cot_ref[...], 0, 0)
    grad = (grad * gelu_slope(pre_ref[...])).astype(bfloat)
    out_ref[...] = grad
    sum_ref[...] = jnp.sum(grad.astype(single), axis=1, keepdims=True)


def grad_pre_of(full_down, cotangent, pre_active):
    width, ff = full_down.shape
    length = cotangent.shape[1]
    tile = 640
    return pl.pallas_call(
        grad_pre_kernel,
        grid=(-(-ff // tile),),
        in_specs=[
            pl.BlockSpec((width, tile), lambda i: (0, i)),
            pl.BlockSpec((width, length), lambda i: (0, 0)),
            pl.BlockSpec((tile, length), lambda i: (i, 0)),
        ],
        out_specs=[
            pl.BlockSpec((tile, length), lambda i: (i, 0)),
            pl.BlockSpec((tile, 1), lambda i: (i, 0)),
        ],
        out_shape=[
            jax.ShapeDtypeStruct((ff, length), bfloat),
            jax.ShapeDtypeStruct((ff, 1), single),
        ],
        compiler_params=pltpu.CompilerParams(vmem_limit_bytes=56 * 2**20),
        cost_estimate=NO_COST,
        name="grad_pre",
    )(full_down, cotangent, pre_active)


def grad_middle_kernel(
    w_ref, grad_ref, normal_ref, scale_ref, gain_ref, cot_ref,
    middle_ref, branch_ref, gain_sum_ref, shift_sum_ref, branch_sum_ref, total_ref,
):
    step = pl.program_id(0)
    tile = w_ref.shape[0]
    place = pl.ds(pl.multiple_of(step * tile, tile), tile)
    total_ref[place, :] = dot(w_ref[...], grad_ref[...], 1, 0)

    @pl.when(step == pl.num_programs(0) - 1)
    def _():
        width, length = total_ref.shape
        rows = width // 4
        z_sum = jnp.zeros((1, length), single)
        zn_sum = jnp.zeros((1, length), single)
        for start in range(0, width, rows):
            at = slice(start, start + rows)
            grad = total_ref[at]
            normal = normal_ref[at]
            product = grad * normal
            gain = gain_ref[at]
            gain_sum_ref[at] = jnp.sum(product, axis=1, keepdims=True)
            shift_sum_ref[at] = jnp.sum(grad, axis=1, keepdims=True)
            z_sum += jnp.sum(grad * gain, axis=0, keepdims=True)
            zn_sum += jnp.sum(product * gain, axis=0, keepdims=True)
        z_mean = z_sum / width
        zn_mean = zn_sum / width
        for start in range(0, width, rows):
            at = slice(start, start + rows)
            z = total_ref[at] * gain_ref[at]
            middle = cot_ref[at].astype(single) + (
                z - z_mean - normal_ref[at] * zn_mean
            ) * scale_ref[...]
            branch = middle.astype(bfloat)
            middle_ref[at] = middle
            branch_ref[at] = branch
            branch_sum_ref[at] = jnp.sum(branch.astype(single), axis=1, keepdims=True)


def grad_middle_of(full_up, grad_pre, normal, scale, gain, cotangent):
    width, ff = full_up.shape
    length = cotangent.shape[1]
    tile = width // 4
    whole = lambda rows, lanes: pl.BlockSpec((rows, lanes), lambda i: (0, 0))
    return pl.pallas_call(
        grad_middle_kernel,
        grid=(width // tile,),
        in_specs=[
            pl.BlockSpec((tile, ff), lambda i: (i, 0)),
            whole(ff, length),
            whole(width, length),
            whole(1, length),
            whole(width, 1),
            whole(width, length),
        ],
        out_specs=[whole(width, length), whole(width, length)] + [whole(width, 1)] * 3,
        out_shape=[
            jax.ShapeDtypeStruct((width, length), single),
            jax.ShapeDtypeStruct((width, length), bfloat),
        ]
        + [jax.ShapeDtypeStruct((width, 1), single)] * 3,
        scratch_shapes=[pltpu.VMEM((width, length), single)],
        compiler_params=pltpu.CompilerParams(vmem_limit_bytes=56 * 2**20),
        cost_estimate=NO_COST,
        name="grad_middle",
    )(full_up, grad_pre, normal, scale, gain, cotangent)


NAMES = (
    "gact", "DAs", "DAk", "UAs", "gn2", "gheads", "DA", "abackA", "UAk", "UBs", "abackB",
    "joinA", "OAs", "UBk", "joinB", "UB", "OAk", "gproj", "OA", "gn1", "UA", "QBs", "QAs",
    "QBk", "QB", "QAk", "QA", "smalls", "S", "asmD", "asmO", "out", "asmU", "asmQ",
)

ORDER = (
    0, 1, 2, 3, 4, 5, 6, 7, 8, 6, 9, 10, 11, 6, 12, 13, 14, 15, 16, 17, 6, 18, 19, 15, 18,
    20, 6, 21, 22, 15, 20, 18, 23, 6, 20, 24, 15, 18, 25, 26, 24, 6, 20, 26, 15, 27, 18, 24,
    20, 26, 28, 18, 15, 20, 24, 26, 29, 18, 28, 15, 24, 28, 26, 30, 24, 20, 26, 28, 24, 28,
    26, 31, 32, 33,
)

ROUTES = {
    "DA": ((0, 1), (1, 0), (2, 2), (3, 3)),
    "UA": ((2, 2), (0, 1), (1, 0), (3, 3)),
    "UB": ((0, 1), (1, 2), (2, 0), (3, 3)),
    "OA": ((1, 0), (0, 1), (2, 2), (3, 3)),
    "QA": ((1, 0), (0, 1), (2, 2), (3, 3)),
    "QB": ((0, 1), (1, 0), (2, 2), (3, 3)),
}

CUTS = {
    "DA": ((0, 1088), (0, 2176)),
    "UA": ((0, 544), (0, 2176)),
    "UB": ((0, 544), (2176, 4352)),
    "OA": ((0, 544), (0, 1088)),
    "QA": ((0, 544), (0, 1664)),
    "QB": ((0, 544), (1664, 3264)),
}

LAYOUTS = {
    "D": [['DA']],
    "U": [['UA', 'UB']],
    "O": [['OA']],
    "Q": [['QA', 'QB']],
}


def normalize(values):
    center = values - jnp.mean(values, axis=0, keepdims=True)
    spread = jnp.mean(center * center, axis=0, keepdims=True)
    scale = lax.rsqrt(spread + epsilon)
    return center * scale, scale


def normalize_back(grad, normal, scale, gain):
    z = grad * gain
    z_mean = jnp.mean(z, axis=0, keepdims=True)
    zn_mean = jnp.mean(z * normal, axis=0, keepdims=True)
    part = (z - z_mean - normal * zn_mean) * scale
    return part, jnp.sum(grad * normal, axis=1), jnp.sum(grad, axis=1)


def tanh_gelu(values):
    return jax.nn.gelu(values, approximate=True)


def shards(
    tokens,
    documents,
    cotangent,
    w_qkv,
    w_out,
    w_up,
    w_down,
    gain_one,
    shift_one,
    bias_query,
    bias_value,
    bias_out,
    gain_two,
    shift_two,
    bias_up,
    bias_down,
):
    at = lax.axis_index("shard")
    first = at == 0
    flag = at.astype(jnp.int32).reshape(1)
    docs = documents[0]
    early_docs = lax.ppermute(docs, "shard", [(0, 1)])

    other_qkv = swapped(w_qkv)
    vectors = jnp.stack(
        [
            gain_one,
            shift_one,
            bias_query,
            bias_value,
            bias_out,
            gain_two,
            shift_two,
            bias_down,
        ]
    )
    other_vectors, other_up_bias = swapped((vectors, bias_up))
    full_out = lax.all_gather(w_out, "shard", axis=0, tiled=True)
    full_up = lax.all_gather(w_up, "shard", axis=0, tiled=True)
    full_down = lax.all_gather(w_down.T, "shard", axis=1, tiled=True)

    def ordered(mine, other, axis):
        return jnp.concatenate(
            [jnp.where(first, mine, other), jnp.where(first, other, mine)], axis=axis
        )

    columns = ordered(vectors, other_vectors, 1).T.astype(single)
    (
        col_gain_one,
        col_shift_one,
        col_query,
        col_value,
        col_out,
        col_gain_two,
        col_shift_two,
        col_down,
    ) = [columns[:, i : i + 1] for i in range(8)]
    col_up = ordered(bias_up, other_up_bias, 0).astype(single)[:, None]

    grad_rows = cotangent[0].T
    width = grad_rows.shape[0]

    rows = tokens[0].T.astype(single)
    normal_one, scale_one = normalize(rows)
    normed_one = (normal_one * col_gain_one + col_shift_one).astype(bfloat)
    normed_one_mine, normed_one_theirs = halves(normed_one, at)
    project = dot(w_qkv, normed_one_mine, 0, 0) + dot(other_qkv, normed_one_theirs, 0, 0)
    col_qkv = jnp.concatenate([col_query, jnp.zeros_like(col_query), col_value], axis=0)
    qkv = (project + col_qkv).astype(bfloat)
    early_kv = lax.ppermute(qkv[width:, SKIP:], "shard", [(0, 1)])

    qkv, early_kv, early_docs, grad_rows, normed_one_theirs = lax.optimization_barrier(
        (qkv, early_kv, early_docs, grad_rows, normed_one_theirs)
    )
    other_grad_rows = swapped(grad_rows)
    normed_one_arrived = swapped(normed_one_theirs)
    heads, lse = attend(flag, docs, early_docs, qkv, early_kv)
    heads_mine, heads_theirs = halves(heads, at)
    heads_arrived = swapped(heads_theirs)
    middle = rows + dot(full_out, heads, 0, 0) + col_out
    normal_two, scale_two = normalize(middle)
    normed_two = (normal_two * col_gain_two + col_shift_two).astype(bfloat)
    normed_two_mine, normed_two_theirs = halves(normed_two, at)
    normed_two, heads_arrived, other_grad_rows, normed_one_arrived = lax.optimization_barrier(
        (normed_two, heads_arrived, other_grad_rows, normed_one_arrived)
    )
    pre_active = dot(full_up, normed_two, 0, 0) + col_up
    active = tanh_gelu(pre_active).astype(bfloat)
    active_mine, active_theirs = halves(active, at)
    active, active_mine, active_theirs, normed_two_theirs, pre_active, grad_rows = (
        lax.optimization_barrier(
            (active, active_mine, active_theirs, normed_two_theirs, pre_active, grad_rows)
        )
    )
    active_arrived = swapped(active_theirs)
    normed_two_arrived = swapped(normed_two_theirs)
    line = Line()
    sums = {name: Sum(line, order) for name, order in ROUTES.items()}
    sums["S"] = SmallSum(line)
    s = State()
    half = width // 2
    ff = pre_active.shape[0]

    def stage_out():
        active_now, middle_now = line.enter(active, middle)
        out = (middle_now + dot(full_down, active_now, 1, 0) + col_down).astype(bfloat)
        line.leave(s.__dict__, output=out)

    operands = {
        "D": ("cot", "cot_other", "active", "active_other"),
        "U": ("normed_two", "normed_two_other", "grad_pre", "grad_pre_other"),
        "O": ("heads", "heads_other", "grad_branch", "grad_branch_other"),
        "Q": ("normed_one", "normed_one_other", "grad_project", "grad_project_other"),
    }
    s.__dict__.update(cot=grad_rows, cot_other=other_grad_rows, active=active_mine)
    s.__dict__.update(active_other=active_arrived, normed_two=normed_two_mine)
    s.__dict__.update(normed_two_other=normed_two_arrived, heads=heads_mine, heads_other=heads_arrived)
    s.__dict__.update(normed_one=normed_one_mine, normed_one_other=normed_one_arrived)

    def pairs_of(name):
        keys = operands[name[0]]
        values = line.enter(*[s.__dict__[key] for key in keys])
        rows, lanes = [slice(*at) for at in CUTS[name]]
        pairs = [(values[i][rows], values[i + 2][lanes]) for i in range(2)]
        return dict(zip(keys, values)), pairs

    def send(name):
        values, pairs = pairs_of(name)
        (sent,) = line.leave(s.__dict__, [sums[name].send(pairs)], **values)
        if not sums[name].plain:
            sums[name].pass_on(sent, sums[name].order[0])

    def keep(name):
        if not sums[name].plain:
            _, pairs = pairs_of(name)
            line.leave(sums[name].__dict__, total=sums[name].keep(pairs))

    def stage_grad_active():
        (cot,) = line.enter(grad_rows)
        grad_pre, bias_sum = grad_pre_of(full_down, cot, pre_active)
        line.leave(s.__dict__, grad_pre=grad_pre, grad_bias_up=bias_sum)
        s.grad_pre_other = swapped(s.grad_pre)

    def stage_normed_two():
        grad_pre, s.normed_two_other = line.enter(s.grad_pre, s.normed_two_other)
        names = "grad_middle", "grad_branch", "grad_gain_two", "grad_shift_two", "grad_bias_out"
        results = grad_middle_of(
            full_up, grad_pre, normal_two, scale_two, col_gain_two, grad_rows
        )
        line.leave(s.__dict__, **dict(zip(names, results)))
        s.grad_branch_other = swapped(s.grad_branch)

    def stage_grad_heads():
        grad_branch, s.grad_branch_other = line.enter(s.grad_branch, s.grad_branch_other)
        line.leave(s.__dict__, grad_heads=dot(full_out, grad_branch, 1, 0).astype(bfloat))

    heads_count = width // HDIM
    ranges = {"A": (0, heads_count // 2), "B": (heads_count // 2, heads_count)}

    def stage_attend_back(name):
        (grad_heads,) = line.enter(s.grad_heads)
        results = attend_back(
            flag, docs, early_docs, qkv, early_kv, grad_heads, heads, lse, *ranges[name]
        )
        back = jnp.concatenate(results[3:], axis=0)
        kept = {name + str(i): one for i, one in enumerate(results[:3])}
        (back,) = line.leave(s.__dict__, [back], **kept)
        s.__dict__["back" + name] = lax.ppermute(back, "shard", [(1, 0)])

    def joined(own, back):
        return (own + jnp.pad(back.astype(single), ((0, 0), (SKIP, 0)))).astype(bfloat)

    def stage_join(name):
        query, key, value, back = line.enter(*[s.__dict__[name + str(i)] for i in range(3)], s.__dict__["back" + name])
        middle_row = back.shape[0] // 2
        key, value = joined(key, back[:middle_row]), joined(value, back[middle_row:])
        line.leave(s.__dict__, **{name + "q": query, name + "k": key, name + "v": value})

    def stage_project():
        pieces = line.enter(*[s.__dict__[name + part] for part in "qkv" for name in "AB"])
        line.leave(s.__dict__, grad_project=jnp.concatenate(pieces, axis=0))
        s.grad_project_other = swapped(s.grad_project)

    def stage_normed_one():
        (grad_project,) = line.enter(s.grad_project)
        grad_normed_one = ordered(
            dot(w_qkv, grad_project, 1, 0), dot(other_qkv, grad_project, 1, 0), 0
        )
        part_one, gain_sum, shift_sum = normalize_back(
            grad_normed_one, normal_one, scale_one, col_gain_one
        )
        line.leave(
            s.__dict__,
            input_grad=(s.grad_middle + part_one).astype(bfloat),
            grad_gain_one=gain_sum,
            grad_shift_one=shift_sum,
        )

    def stage_small():
        bias_out, gain_two_sum, shift_two_sum, bias_up_sum, cot, grad_project = line.enter(
            s.grad_bias_out,
            s.grad_gain_two,
            s.grad_shift_two,
            s.grad_bias_up,
            grad_rows,
            s.grad_project,
        )
        small = jnp.stack(
            [
                s.grad_gain_one,
                s.grad_shift_one,
                jnp.sum(grad_project[:width].astype(single), axis=1),
                jnp.sum(grad_project[2 * width :].astype(single), axis=1),
                bias_out[:, 0],
                gain_two_sum[:, 0],
                shift_two_sum[:, 0],
                jnp.sum(cot.astype(single), axis=1),
            ]
        )
        lanes = ff // 2 // half
        up_parts = bias_up_sum[:, 0].reshape(2, lanes, half)
        lower = jnp.concatenate([small[:, :half], up_parts[0]], axis=0)
        upper = jnp.concatenate([small[:, half:], up_parts[1]], axis=0)
        sums["S"].send(jnp.where(first, lower, upper), jnp.where(first, upper, lower))

    grads = {}

    def assemble(matrix):
        grads[matrix] = assembled(line, [[sums[name] for name in row] for row in LAYOUTS[matrix]])

    stages = {
        "out": stage_out,
        "gact": stage_grad_active,
        "gn2": stage_normed_two,
        "gheads": stage_grad_heads,
        "abackA": lambda: stage_attend_back("A"),
        "abackB": lambda: stage_attend_back("B"),
        "joinA": lambda: stage_join("A"),
        "joinB": lambda: stage_join("B"),
        "gproj": stage_project,
        "gn1": stage_normed_one,
        "smalls": stage_small,
    }
    for name in CUTS:
        stages[name + "s"] = functools.partial(send, name)
        stages[name + "k"] = functools.partial(keep, name)
    last = []
    for name in [NAMES[i] for i in ORDER]:
        if name in stages:
            stages[name]()
        elif name in sums:
            sums[name].step()
        else:
            last.append(name[-1])
            for one in sums.values():
                while len(last) == len(LAYOUTS) and not one.finished():
                    one.step()
            if all(sums[one].finished() for row in LAYOUTS[last[-1]] for one in row):
                assemble(last[-1])
    for matrix in LAYOUTS:
        if matrix not in grads:
            assemble(matrix)
    while not sums["S"].finished():
        sums["S"].step()
    small = sums["S"].total
    return (
        s.output.T[None],
        s.input_grad.T[None],
        grads["Q"],
        grads["O"],
        grads["U"],
        grads["D"].T,
        small[0],
        small[1],
        small[2],
        small[3],
        small[4],
        small[5],
        small[6],
        small[8:].reshape(-1),
        small[7],
    )


def solution(mesh):
    sequences = P("replica", "shard", None)
    matrix = P("shard", None)
    vector = P("shard")
    return jax.shard_map(
        shards,
        mesh=mesh,
        in_specs=(sequences, P("replica", "shard"), sequences) + (matrix,) * 4 + (vector,) * 9,
        out_specs=(sequences, sequences) + (matrix,) * 4 + (vector,) * 9,
        check_vma=False,
    )
```
